128 devices in a mesh: base: 8 (over z, core), grp: 16 (over y, x).
Axes of the slice: x: 4, y: 4, z: 4, core: 2. Of those that a mesh axis runs over, the one named last changes fastest.
Arguments:
- q_blocks: bfloat16 [8192, 8, 128, 128], P(('base', 'grp')), may hold values from -0.1875 to 0.1875
- p_blocks: bfloat16 [8192, 16, 128], P(('base', 'grp')), may hold values from -2 to 2
- col_index: int32 [8192, 8], P(('base', 'grp')), may hold values from 0 to 3071, as said below
- agg_of_block: int32 [8192, 1], P(('base', 'grp')), may hold values from 0 to 63; in each aligned block of 64 rows (0 to 63, 64 to 127, ...) at most 2 rows name the same one
Outputs:
- qp_product: float32 [8192, 16, 128], P(('base', 'grp'))
- coarse_rows: float32 [512, 16, 3072], P(('base', 'grp'))
The draws below stay inside these ranges and needn't reach their ends.
Inputs may be any that keep to these rules, and one draw needn't show every extreme that they name: `col_index`: slot 0 names the row's own block. Slots below 6 have base offset 1 and name a block held by the same grp index or the one just below or above it (cyclically); the other slots have base offset 0 or 2 and name a block held by the same grp index. `agg_of_block`: among the 64 block rows of one device no aggregate occurs more than 2 times, and that count is reached.
All inputs are finite; a program needn't handle non-finite values.
Results may differ from the reference program's by a relative error of at most 0.0003.
Values may be sent and summed in bfloat16 or wider, within the bound.
A program may use at most 128 MiB of HBM per device.

```python
import math
import jax
import jax.numpy as jnp
import numpy as np
from jax import lax

B = 128
K = 16
NB = 8
NB_IN = 6
MOST = 2
R = 64
AGGB = 64
BLOCKS = 8192
N_BASE = 8
N_GRP = 16


def draw_col_index(key, part):
    rows = N_BASE * N_GRP * R
    index = jnp.arange(rows, dtype=jnp.int32)
    grp_pos = index // R % N_GRP
    local = index % R
    key_a, key_b, key_c, key_d = jax.random.split(key, 4)
    offset = jax.random.randint(key_a, (rows, NB_IN), -1, 2)
    device = (grp_pos[:, None] + offset) % N_GRP
    within = jax.random.randint(key_b, (rows, NB_IN), 0, R)
    inner = device * R + within
    inner = inner.at[:, 0].set(grp_pos * R + local)
    inner = inner + R * N_GRP
    side = 2 * jax.random.randint(key_c, (rows, NB - NB_IN), 0, 2)
    near = jax.random.randint(key_d, (rows, NB - NB_IN), 0, R)
    outer = side * (R * N_GRP) + grp_pos[:, None] * R + near
    return jnp.concatenate([inner, outer], axis=1).astype(jnp.int32)


def steps_of(stream_key, shape, cuts, low, high):
    level = 1.0
    for dim, shards_of in cuts:
        steps = jax.random.uniform(jax.random.fold_in(jax.random.fold_in(stream_key, 6), dim), (shards_of,), jnp.float32, low / len(cuts), high / len(cuts))
        level = level * jnp.repeat(jnp.exp(steps), shape[dim] // shards_of).reshape((-1,) + (1,) * (len(shape) - 1 - dim))
    return level


def deal_out(stream_key, own, number, rows, amount, top, bound, slope):
    ranking = jax.random.permutation(stream_key, amount)
    crowded, ordinary = load_shares(amount, rows * top, bound, slope, True), load_shares(amount, rows * top, bound, slope, False)
    places = jnp.arange(amount)

    def named(lengths, offset_by):
        used = int((lengths > 0).sum())
        fixed = max(1, used // 4)
        shifted = fixed + (places - fixed + offset_by * (used - fixed)) % max(1, amount - fixed)
        return jnp.zeros((amount,), jnp.int32).at[ranking[jnp.where(places < fixed, places, shifted)]].set(jnp.asarray(lengths, jnp.int32))

    lengths = jnp.where(number % 4 == 0, named(crowded, number // 4), named(ordinary, number - number // 4 - 1))
    mixed = jax.random.permutation(jax.random.fold_in(own, 3), amount)
    source_of, sink = mixed[0:amount // 2 * 2:2], mixed[1:amount // 2 * 2:2]
    margin = jnp.minimum(lengths[source_of] - 1, bound - lengths[sink]) // 2
    margin = jnp.where((source_of == ranking[0]) | (sink == ranking[0]) | (lengths[sink] == 0), 0, jnp.maximum(margin, 0))
    shifted = jax.random.randint(jax.random.fold_in(own, 4), (amount // 2,), 0, 1 << 20) % (margin + 1)
    lengths = lengths.at[source_of].add(-shifted).at[sink].add(shifted)
    labels = jnp.searchsorted(jnp.cumsum(lengths), jnp.arange(rows * top), side="right").astype(jnp.int32)
    listing = labels.reshape(top, rows).T
    listing = listing[jax.random.permutation(jax.random.fold_in(own, 1), rows)]
    offset_by = jax.random.randint(jax.random.fold_in(own, 2), (rows, 1), 0, top)
    return jnp.take_along_axis(listing, (jnp.arange(top)[None, :] + offset_by) % top, axis=1)


def load_shares(amount, total, most, skew, full):
    portions = [(1 << 20) // math.isqrt(standing ** skew) + 1 for standing in range(1, amount + 1)]
    largest = most if full else min(most, max(-(-total // amount), total * portions[0] // sum(portions)))
    least = 1 if total - largest >= amount - 1 else 0
    given, rest = [largest] + [least] * (amount - 1), total - largest - least * (amount - 1)
    while rest > 0:
        candidates = [i for i in range(1, amount) if given[i] < largest] or [i for i in range(1, amount) if given[i] < most]
        pool, remaining = sum([portions[i] for i in candidates]), rest
        for i in candidates:
            more = min(most - given[i], max(1, remaining * portions[i] // pool), rest)
            given[i] = given[i] + more
            rest = rest - more
    return np.array(given)


def bell_draw(stream_key, dims, deviation, most, shards=(), kind=jnp.bfloat16):
    values = deviation * jax.random.normal(stream_key, dims, jnp.float32)
    if shards:
        values = values * steps_of(stream_key, dims, shards, -0.22, 0.18)
    return jnp.clip(values, -most, most).astype(kind)


def setup_inputs(seed: int = 0) -> dict:
    key_list = jax.random.split(jax.random.key(seed), 5)
    q_blocks = bell_draw(key_list[0], (BLOCKS, NB, B, B), (NB * B) ** -0.5, 0.1875, ((0, 128),))
    p_blocks = bell_draw(key_list[1], (BLOCKS, K, B), 0.3, 2.0, ((0, 128),))
    col_index = draw_col_index(jax.random.fold_in(key_list[4], 71), 0)
    agg_of_block_keys = jax.random.split(jax.random.fold_in(key_list[3], 1), BLOCKS // R)
    agg_of_block_turns = jax.random.permutation(jax.random.fold_in(key_list[3], 3), BLOCKS // R)
    agg_of_block = jax.vmap(lambda own, number: deal_out(jax.random.fold_in(key_list[3], 2), own, number, R, AGGB, 1, MOST, 1))(agg_of_block_keys, agg_of_block_turns).reshape((BLOCKS, 1))
    return {"q_blocks": q_blocks, "p_blocks": p_blocks, "col_index": col_index, "agg_of_block": agg_of_block}


def reference(q_blocks, p_blocks, col_index, agg_of_block):
    group = N_GRP * R
    p_four = p_blocks.reshape(N_BASE, group, K, B)
    agg_two = agg_of_block.reshape(N_BASE, group)
    q_five = q_blocks.reshape(N_BASE, group, NB, B, B)
    c_three = col_index.reshape(N_BASE, group, NB)
    hp = lax.Precision.HIGHEST

    def one_base(base_id):
        before = (base_id - 1) % N_BASE
        after = (base_id + 1) % N_BASE
        table = jnp.concatenate([p_four[before], p_four[base_id], p_four[after]], axis=0)
        agg_table = jnp.concatenate([agg_two[before], agg_two[base_id], agg_two[after]], axis=0)
        columns = c_three[base_id]
        picked = table[columns]
        colagg = agg_table[columns] + (columns // group) * AGGB
        vals = jnp.einsum("inkc,inbc->inkb", picked.astype(jnp.float32), q_five[base_id].astype(jnp.float32))
        product = jnp.sum(vals, axis=1)
        wts = jnp.einsum("ikb,inlb->inkl", p_four[base_id].astype(jnp.float32), vals, precision=hp)
        one_col = (colagg[:, :, None] == jnp.arange(3 * AGGB, dtype=jnp.int32)[None, None, :]).astype(jnp.float32)
        one_row = (agg_two[base_id][:, None] == jnp.arange(AGGB, dtype=jnp.int32)[None, :]).astype(jnp.float32)
        mixed = jnp.einsum("inc,inkl->ickl", one_col, wts, precision=hp)
        coarse = jnp.einsum("ia,ickl->akcl", one_row, mixed, precision=hp)
        return product, coarse.reshape(AGGB, K, 3 * AGGB * K)

    products, coarse = lax.map(one_base, jnp.arange(N_BASE, dtype=jnp.int32))
    return products.reshape(N_BASE * group, K, B), coarse.reshape(N_BASE * AGGB, K, 3 * AGGB * K)
```

```python
import functools

import jax
import jax.numpy as jnp
from jax import lax
from jax.experimental import pallas as pl
from jax.experimental.pallas import tpu as pltpu
from jax.sharding import PartitionSpec as P

F32, BF16, I32 = jnp.float32, jnp.bfloat16, jnp.int32
MESH = pl.DeviceIdType.MESH
R, NB, NB_IN, K, B = 64, 8, 6, 16, 128
N_BASE, N_GRP = 8, 16
OWN = 4
SLOTS = 2 * OWN
CH = 24
PAIRS = ((6, 7), (0, 1), (2, 3), (4, 5))


def dot_t(a, b):
    return lax.dot_general(a, b, (((1,), (1,)), ((), ())), preferred_element_type=F32)


def iota(shape, dim):
    return lax.broadcasted_iota(I32, shape, dim)


def product_kernel(
    col_s, col_v, agg_v, q_hbm, p_hbm,
    prod, w_in, meta_in,
    q_v, near, side, aggtab, pos, split, w_v, pack, meta, order_v, order_s,
    q_sem, own_sem, p_send, p_recv, a_send, a_recv, w_send, w_recv, m_send, m_recv, loc_sem,
):
    base, grp = lax.axis_index("base"), lax.axis_index("grp")
    sends = (
        ({"grp": (grp + 1) % N_GRP}, near, 0, 0),
        ({"grp": (grp + N_GRP - 1) % N_GRP}, near, 2, 2),
        ({"base": (base + 1) % N_BASE}, side, 0, 3),
        ({"base": (base + N_BASE - 1) % N_BASE}, side, 1, 4),
    )
    q_copies = [
        pltpu.make_async_copy(q_hbm.at[:, pl.ds(a, 2)], q_v.at[:, pl.ds(a, 2)], q_sem.at[c])
        for c, (a, _) in enumerate(PAIRS)
    ]
    own_copy = pltpu.make_async_copy(p_hbm, near.at[pl.ds(R, R)], own_sem)
    own_copy.start()
    barrier = pltpu.get_barrier_semaphore()
    for d in range(1, N_GRP):
        pl.semaphore_signal(barrier, 1, device_id={"grp": (grp + d) % N_GRP}, device_id_type=MESH)
    for d in (1, N_BASE - 1):
        pl.semaphore_signal(barrier, 1, device_id={"base": (base + d) % N_BASE}, device_id_type=MESH)
    for c in q_copies:
        c.start()

    row, lane = iota((R, B), 0), iota((R, B), 1)
    agg_col = agg_v[...].astype(F32)
    agg_row = jnp.sum(jnp.where(row == lane, agg_col, 0.0), axis=0, keepdims=True)
    aggtab[1] = jnp.broadcast_to(agg_row, (8, B))

    pl.semaphore_wait(barrier, N_GRP + 1)
    p_copies, a_copies = [], []
    for s, (to, tab, part, seg) in enumerate(sends):
        p_copies.append(
            pltpu.make_async_remote_copy(
                p_hbm, tab.at[pl.ds(part * R, R)], p_send.at[s], p_recv.at[s], device_id=to, device_id_type=MESH
            )
        )
        a_copies.append(
            pltpu.make_async_remote_copy(
                aggtab.at[1], aggtab.at[seg], a_send.at[s], a_recv.at[s], device_id=to, device_id_type=MESH
            )
        )
    for c in p_copies + a_copies:
        c.start()

    before = (agg_col == agg_row) & (lane < row)
    rank = jnp.sum(jnp.where(before, 1.0, 0.0), axis=1, keepdims=True)
    match = (2.0 * agg_col + rank) == lane.astype(F32)
    order = jnp.sum(jnp.where(match, row.astype(F32), 0.0), axis=0, keepdims=True)
    order_v[...] = jnp.broadcast_to(order, (8, B)).astype(I32)
    order_copy = pltpu.make_async_copy(order_v, order_s, loc_sem.at[0])
    order_copy.start()

    def position(c, slot):
        if slot >= NB_IN:
            return (c >> 11) * R + (c & (R - 1))
        shard = jnp.minimum(((c >> 6) - grp + 1) & (N_GRP - 1), 2)
        return shard * R + (c & (R - 1))

    @pl.loop(0, R)
    def _(i):
        for n in range(NB):
            pos[i, n] = position(col_s[i, n], n)

    def values(pair, i):
        a, b = pair
        tab = side if a >= NB_IN else near
        zero = jnp.zeros((K, B), BF16)
        left, right = [], []
        for d in range(2):
            left += [tab[pos[i + d, a]], zero]
            right += [zero, tab[pos[i + d, b]]]
        lhs = jnp.concatenate([jnp.concatenate(left, 0), jnp.concatenate(right, 0)], 1)
        rhs = jnp.concatenate([jnp.concatenate([q_v[i + d, a], q_v[i + d, b]], 1) for d in range(2)], 0)
        out = dot_t(lhs, rhs)
        sums = []
        for d in range(2):
            v = out[2 * d * K : 2 * (d + 1) * K, d * B : (d + 1) * B]
            high = v.astype(BF16)
            split[i + d, a * K : (a + 2) * K, :B] = high
            split[i + d, a * K : (a + 2) * K, B:] = (v - high.astype(F32)).astype(BF16)
            sums.append(v[:K] + v[K:])
        return sums

    own_copy.wait()
    for s in (2, 3):
        p_copies[s].wait_recv()
    q_copies[0].wait()

    @pl.loop(0, R // 16)
    def _(j):
        for u in range(0, 16, 2):
            i = j * 16 + u
            for d, v in enumerate(values(PAIRS[0], i)):
                prod[i + d] = v

    for c in a_copies:
        c.wait_recv()
    col = col_v[...]
    colagg = jnp.where(lane == NB, 1.0, 0.0)
    for n in range(NB):
        at = position(col[:, n : n + 1], n)
        found = jnp.zeros((R, B), F32)
        for part, seg in enumerate((3, 4) if n >= NB_IN else (0, 1, 2)):
            found = found + jnp.where(at - part * R == lane, aggtab[seg, 0:1], 0.0)
        total = jnp.sum(found, axis=1, keepdims=True) + ((col[:, n : n + 1] >> 10) * R).astype(F32)
        colagg = jnp.where(lane == n, total, colagg)
    placed = lax.dot_general(
        jnp.where(match, 1.0, 0.0).astype(BF16), colagg.astype(BF16), (((0,), (0,)), ((), ())),
        preferred_element_type=F32,
    )
    meta[...] = placed.astype(I32).reshape(N_GRP, SLOTS, B)

    for s in (0, 1):
        p_copies[s].wait_recv()
    for c in q_copies[1:]:
        c.wait()

    @pl.loop(0, R // 16)
    def _(j):
        for u in range(0, 16, 2):
            i = j * 16 + u
            all_sums = [values(pair, i) for pair in PAIRS[1:]]
            for d in range(2):
                prod[i + d] += all_sums[0][d] + all_sums[1][d] + all_sums[2][d]

    @pl.loop(0, R // 16)
    def _(j):
        for u in range(0, 16, 2):
            i = j * 16 + u
            p_two = near[pl.ds(R + i, 2)].reshape(2 * K, B)
            out = dot_t(jnp.concatenate([p_two, p_two], 1), split[pl.ds(i, 2)].reshape(2 * B, 2 * B))
            w_v[i] = out[:K, :B]
            w_v[i + 1] = out[K:, B:]

    order_copy.wait()

    def gathered(d, to):
        for t in range(SLOTS):
            pack[d, t] = w_v[order_s[0, to * SLOTS + t] & (R - 1)]

    copies = []
    for d in range(1, N_GRP):
        to = (grp + d) % N_GRP
        gathered(d, to)
        for src, dst, send, recv in (
            (pack.at[d], w_in.at[grp], w_send, w_recv),
            (meta.at[to], meta_in.at[grp], m_send, m_recv),
        ):
            copies.append(
                pltpu.make_async_remote_copy(
                    src, dst, send.at[d], recv.at[d], device_id={"grp": to}, device_id_type=MESH
                )
            )
            copies[-1].start()
    gathered(0, grp)
    w_own = pltpu.make_async_copy(pack.at[0], w_in.at[grp], loc_sem.at[1])
    m_own = pltpu.make_async_copy(meta.at[grp], meta_in.at[grp], loc_sem.at[2])
    w_own.start()
    m_own.start()
    for c in p_copies + a_copies:
        c.wait_send()
    w_own.wait()
    m_own.wait()
    for c in copies:
        c.wait()


def coarse_kernel(meta, w, prod_in, coarse, prod_out, acc0, acc1, acc2, acc3, sem):
    copy = pltpu.make_async_copy(prod_in, prod_out, sem)
    copy.start()
    accs = (acc0, acc1, acc2, acc3)
    for acc in accs:
        acc[...] = jnp.zeros_like(acc)
    group = iota((K, B), 1) >> 4

    @pl.loop(0, N_GRP)
    def _(src):
        for t in range(2):
            for n in range(NB):
                for a, acc in enumerate(accs):
                    s = 2 * a + t
                    c = meta[src, s, n]
                    low = c & 7
                    turned = pltpu.roll(w[src, s], ((low - n) & 7) * K, 1)
                    here = jnp.where(meta[src, s, NB] == 1, low, -1)
                    acc[c >> 3] += jnp.where(group == here, turned, 0.0)

    for a, acc in enumerate(accs):
        for h in range(CH):
            coarse[a, :, h * B : (h + 1) * B] = acc[h]
    copy.wait()


def on_device(q_blocks, p_blocks, col_index, agg_of_block):
    vmem, smem = pl.BlockSpec(memory_space=pltpu.VMEM), pl.BlockSpec(memory_space=pltpu.SMEM)
    any_ = pl.BlockSpec(memory_space=pl.ANY)
    dma = pltpu.SemaphoreType.DMA
    prod, w_in, meta_in = pl.pallas_call(
        product_kernel,
        in_specs=[smem, vmem, vmem, any_, any_],
        out_specs=[vmem, any_, any_],
        out_shape=[
            jax.ShapeDtypeStruct((R, K, B), F32),
            jax.ShapeDtypeStruct((N_GRP, SLOTS, K, B), F32),
            jax.ShapeDtypeStruct((N_GRP, SLOTS, B), I32),
        ],
        scratch_shapes=[
            pltpu.VMEM((R, NB, B, B), BF16),
            pltpu.VMEM((3 * R, K, B), BF16),
            pltpu.VMEM((2 * R, K, B), BF16),
            pltpu.VMEM((5, 8, B), F32),
            pltpu.SMEM((R, NB), I32),
            pltpu.VMEM((R, B, 2 * B), BF16),
            pltpu.VMEM((R, K, B), F32),
            pltpu.VMEM((N_GRP, SLOTS, K, B), F32),
            pltpu.VMEM((N_GRP, SLOTS, B), I32),
            pltpu.VMEM((8, B), I32),
            pltpu.SMEM((8, B), I32),
            dma((4,)),
            dma,
            dma((4,)),
            dma((4,)),
            dma((4,)),
            dma((4,)),
            dma((N_GRP,)),
            dma((N_GRP,)),
            dma((N_GRP,)),
            dma((N_GRP,)),
            dma((3,)),
        ],
        compiler_params=pltpu.CompilerParams(
            collective_id=0, has_side_effects=True, vmem_limit_bytes=40 << 20
        ),
        name="products",
    )(col_index, col_index, agg_of_block, q_blocks, p_blocks)
    coarse, product = pl.pallas_call(
        coarse_kernel,
        in_specs=[smem, vmem, any_],
        out_specs=[vmem, any_],
        out_shape=[
            jax.ShapeDtypeStruct((OWN, K, CH * B), F32),
            jax.ShapeDtypeStruct((R, K, B), F32),
        ],
        scratch_shapes=[pltpu.VMEM((CH, K, B), F32)] * OWN + [dma],
        compiler_params=pltpu.CompilerParams(vmem_limit_bytes=16 << 20),
        name="coarse",
    )(meta_in, w_in, prod)
    return product, coarse


def solution(mesh):
    placed = (
        P(("base", "grp"), None, None, None),
        P(("base", "grp"), None, None),
        P(("base", "grp"), None),
        P(("base", "grp"), None),
    )
    return jax.shard_map(
        on_device,
        mesh=mesh,
        in_specs=placed,
        out_specs=(P(("base", "grp"), None, None), P(("base", "grp"), None, None)),
        check_vma=False,
    )
```

```python
import functools

import jax
import jax.numpy as jnp
from jax import lax
from jax.experimental import pallas as pl
from jax.experimental.pallas import tpu as pltpu
from jax.sharding import PartitionSpec as P

F32, BF16, I32 = jnp.float32, jnp.bfloat16, jnp.int32
MESH = pl.DeviceIdType.MESH
R, NB, NB_IN, K, B = 64, 8, 6, 16, 128
N_BASE, N_GRP = 8, 16
OWN = 4
SLOTS = 2 * OWN
STEPS = 32000.0
CH = 24
PAIRS = ((6, 7), (0, 1), (2, 3), (4, 5))


def dot_t(a, b):
    return lax.dot_general(a, b, (((1,), (1,)), ((), ())), preferred_element_type=F32)


def iota(shape, dim):
    return lax.broadcasted_iota(I32, shape, dim)


def product_kernel(
    col_hbm, agg_hbm, q_hbm, p_hbm,
    prod, w_in, meta_in,
    q_v, near, side, col_s, col_v, agg_v, aggtab, split, w_v, pack, info, meta, order_v, order_s,
    q_sem, loc_sem, p_send, p_recv, a_send, a_recv, w_send, w_recv, m_send, m_recv,
):
    base, grp = lax.axis_index("base"), lax.axis_index("grp")
    barrier = pltpu.get_barrier_semaphore()
    for d in range(1, N_GRP):
        pl.semaphore_signal(barrier, 1, device_id={"grp": (grp + d) % N_GRP}, device_id_type=MESH)
    for d in (1, N_BASE - 1):
        pl.semaphore_signal(barrier, 1, device_id={"base": (base + d) % N_BASE}, device_id_type=MESH)
    sends = (
        ({"grp": (grp + 1) % N_GRP}, near, 0, 0),
        ({"grp": (grp + N_GRP - 1) % N_GRP}, near, 2, 2),
        ({"base": (base + 1) % N_BASE}, side, 0, 3),
        ({"base": (base + N_BASE - 1) % N_BASE}, side, 1, 4),
    )
    agg_copy = pltpu.make_async_copy(agg_hbm, agg_v, loc_sem.at[0])
    col_copies = (
        pltpu.make_async_copy(col_hbm, col_s, loc_sem.at[1]),
        pltpu.make_async_copy(col_hbm, col_v, loc_sem.at[2]),
    )
    own_copy = pltpu.make_async_copy(p_hbm, near.at[pl.ds(R, R)], loc_sem.at[3])
    for c in (agg_copy, *col_copies, own_copy):
        c.start()
    q_copies = [
        pltpu.make_async_copy(q_hbm.at[:, pl.ds(a, 2)], q_v.at[:, pl.ds(a, 2)], q_sem.at[c])
        for c, (a, _) in enumerate(PAIRS)
    ]
    for c in q_copies:
        c.start()

    row, lane = iota((R, B), 0), iota((R, B), 1)
    agg_copy.wait()
    agg_row = jnp.concatenate([agg_v[...], jnp.zeros((1, B - R), I32)], 1).astype(F32)
    aggtab[1] = jnp.broadcast_to(agg_row, (8, B))

    pl.semaphore_wait(barrier, N_GRP + 1)
    p_copies, a_copies = [], []
    for s, (to, tab, part, seg) in enumerate(sends):
        p_copies.append(
            pltpu.make_async_remote_copy(
                p_hbm, tab.at[pl.ds(part * R, R)], p_send.at[s], p_recv.at[s], device_id=to, device_id_type=MESH
            )
        )
        a_copies.append(
            pltpu.make_async_remote_copy(
                aggtab.at[1], aggtab.at[seg], a_send.at[s], a_recv.at[s], device_id=to, device_id_type=MESH
            )
        )
    for c in a_copies + p_copies:
        c.start()

    agg_col = jnp.sum(jnp.where(row == lane, agg_row, 0.0), axis=1, keepdims=True)
    before = (agg_col == agg_row) & (lane < row)
    rank = jnp.sum(jnp.where(before, 1.0, 0.0), axis=1, keepdims=True)
    match = (2.0 * agg_col + rank) == lane.astype(F32)
    order = jnp.sum(jnp.where(match, row.astype(F32), 0.0), axis=0, keepdims=True)
    order_v[...] = jnp.broadcast_to(order, (8, B)).astype(I32)
    order_copy = pltpu.make_async_copy(order_v, order_s, loc_sem.at[4])
    order_copy.start()

    def position(c, slot):
        if slot >= NB_IN:
            return (c >> 11) * R + (c & (R - 1))
        shard = jnp.minimum(((c >> 6) - grp + 1) & (N_GRP - 1), 2)
        return shard * R + (c & (R - 1))

    def values(pair, i):
        a, b = pair
        tab = side if a >= NB_IN else near
        zero = jnp.zeros((K, B), BF16)
        left, right = [], []
        for d in range(2):
            left += [tab[position(col_s[a, i + d], a)], zero]
            right += [zero, tab[position(col_s[b, i + d], b)]]
        lhs = jnp.concatenate([jnp.concatenate(left, 0), jnp.concatenate(right, 0)], 1)
        rhs = jnp.concatenate([jnp.concatenate([q_v[i + d, a], q_v[i + d, b]], 1) for d in range(2)], 0)
        out = dot_t(lhs, rhs)
        sums = []
        for d in range(2):
            v = out[2 * d * K : 2 * (d + 1) * K, d * B : (d + 1) * B]
            high = v.astype(BF16)
            split[i + d, a * K : (a + 2) * K, :B] = high
            split[i + d, a * K : (a + 2) * K, B:] = (v - high.astype(F32)).astype(BF16)
            sums.append(v[:K] + v[K:])
        return sums

    for c in col_copies:
        c.wait()
    for c in a_copies:
        c.wait_recv()
    col = jnp.concatenate([col_v[...], jnp.zeros((NB, B - R), I32)], 1)
    near_at, side_at = position(col, 0), position(col, NB_IN)

    def looked_up(low, high, at):
        table = jnp.concatenate([aggtab[low][:, :R], aggtab[high][:, :R]], 1)
        return jnp.take_along_axis(table, at, axis=1)

    inner = jnp.where(near_at < B, looked_up(0, 1, near_at & (B - 1)), looked_up(2, 2, near_at & (B - 1)))
    outer = looked_up(3, 4, side_at & (B - 1))
    colagg = jnp.where(iota((NB, B), 0) < NB_IN, inner, outer) + ((col >> 10) * R).astype(F32)
    info[...] = jnp.zeros_like(info)
    info[:NB] = colagg
    info[NB : NB + 1] = jnp.ones((1, B), F32)

    own_copy.wait()
    for s in (2, 3):
        p_copies[s].wait_recv()
    q_copies[0].wait()

    @pl.loop(0, R // 16)
    def _(j):
        for u in range(0, 16, 2):
            i = j * 16 + u
            for d, v in enumerate(values(PAIRS[0], i)):
                prod[i + d] = v

    for s in (0, 1):
        p_copies[s].wait_recv()
    for c in q_copies[1:]:
        c.wait()

    @pl.loop(0, R // 16)
    def _(j):
        for u in range(0, 16, 2):
            i = j * 16 + u
            all_sums = [values(pair, i) for pair in PAIRS[1:]]
            for d in range(2):
                prod[i + d] += all_sums[0][d] + all_sums[1][d] + all_sums[2][d]

    spot = iota((K, B), 1)

    @pl.loop(0, R // 16)
    def _(j):
        widths = info[K : 2 * K]
        for u in range(0, 16, 2):
            i = j * 16 + u
            p_two = near[pl.ds(R + i, 2)].reshape(2 * K, B)
            out = dot_t(jnp.concatenate([p_two, p_two], 1), split[pl.ds(i, 2)].reshape(2 * B, 2 * B))
            for d in range(2):
                w = out[d * K : (d + 1) * K, d * B : (d + 1) * B]
                most = jnp.max(jnp.abs(w), axis=1, keepdims=True)
                width = jnp.maximum(1.01 * most, 1e-30).astype(BF16).astype(F32)
                w_v[i + d] = jnp.round(w * (STEPS / width)).astype(I32).astype(jnp.int16)
                widths = jnp.where(spot == i + d, width, widths)
        info[K : 2 * K] = widths

    meta[...] = lax.dot_general(
        jnp.where(match, 1.0, 0.0).astype(BF16), info[:, :R].astype(BF16), (((0,), (1,)), ((), ())),
        preferred_element_type=F32,
    ).reshape(N_GRP, SLOTS, B)
    order_copy.wait()

    def gathered(d, to):
        for t in range(SLOTS):
            pack[d, t] = w_v[order_s[0, to * SLOTS + t] & (R - 1)]

    copies = []
    for d in range(1, N_GRP):
        to = (grp + d) % N_GRP
        gathered(d, to)
        for src, dst, send, recv in (
            (pack.at[d], w_in.at[grp], w_send, w_recv),
            (meta.at[to], meta_in.at[grp], m_send, m_recv),
        ):
            copies.append(
                pltpu.make_async_remote_copy(
                    src, dst, send.at[d], recv.at[d], device_id={"grp": to}, device_id_type=MESH
                )
            )
            copies[-1].start()
    gathered(0, grp)
    w_own = pltpu.make_async_copy(pack.at[0], w_in.at[grp], loc_sem.at[5])
    m_own = pltpu.make_async_copy(meta.at[grp], meta_in.at[grp], loc_sem.at[6])
    w_own.start()
    m_own.start()
    for c in p_copies + a_copies:
        c.wait_send()
    w_own.wait()
    m_own.wait()
    for c in copies:
        c.wait()


def coarse_kernel(
    meta, w, prod_in, coarse, prod_out, acc0, acc1, acc2, acc3, place_v, place_s, listed, count, sem
):
    copy = pltpu.make_async_copy(prod_in, prod_out, sem.at[0])
    copy.start()
    accs = (acc0, acc1, acc2, acc3)
    turned = meta[...].T
    widths = turned[K : 2 * K] * (1.0 / STEPS)
    slot = iota((K, B), 0)
    col = turned[:K].astype(I32)
    low = col & 7
    taken = (turned[NB : NB + 1] > 0.5) & (slot < NB)
    place_v[...] = jnp.where(taken, ((col >> 3) << 8) | (((low - slot) & 7) << 4) | low, 15)
    place_copy = pltpu.make_async_copy(place_v, place_s, sem.at[1])
    place_copy.start()
    for a, acc in enumerate(accs):
        acc[...] = jnp.zeros_like(acc)
        count[a] = 0
    place_copy.wait()

    @pl.loop(0, N_GRP)
    def _(src):
        for s in range(SLOTS):
            a, e = s // 2, src * SLOTS + s
            had = count[a]
            listed[a, had] = e
            count[a] = had + jnp.where(place_s[0, e] == 15, 0, 1)

    most = functools.reduce(jnp.maximum, [count[a] for a in range(OWN)])
    for a in range(OWN):

        @pl.loop(count[a], most)
        def _(j):
            listed[a, j] = B

    group = iota((K, B), 1) >> 4

    @pl.loop(0, most)
    def _(j):
        rows = []
        for a in range(OWN):
            code = listed[a, j]
            e = code & (B - 1)
            width = pltpu.roll(widths, (B - e) & (B - 1), 1)[:, :1]
            rows.append((e, (code >> 7) * NB, w[e].astype(I32).astype(F32) * width))
        for n in range(NB):
            for acc, (e, skip, x) in zip(accs, rows):
                place = place_s[n + skip, e]
                acc[place >> 8] += jnp.where(group == (place & 15), pltpu.roll(x, place & 0x70, 1), 0.0)

    for a, acc in enumerate(accs):
        for h in range(CH):
            coarse[a, :, h * B : (h + 1) * B] = acc[h]
    copy.wait()


def on_device(q_blocks, p_blocks, col_index, agg_of_block):
    vmem, hbm, any_ = (pl.BlockSpec(memory_space=m) for m in (pltpu.VMEM, pltpu.HBM, pl.ANY))
    dma = pltpu.SemaphoreType.DMA
    prod, w_in, meta_in = pl.pallas_call(
        product_kernel,
        in_specs=[hbm] * 4,
        out_specs=[vmem, any_, any_],
        out_shape=[
            jax.ShapeDtypeStruct((R, K, B), F32),
            jax.ShapeDtypeStruct((N_GRP, SLOTS, K, B), jnp.int16),
            jax.ShapeDtypeStruct((N_GRP, SLOTS, B), F32),
        ],
        scratch_shapes=[
            pltpu.VMEM((R, NB, B, B), BF16),
            pltpu.VMEM((3 * R, K, B), BF16),
            pltpu.VMEM((2 * R, K, B), BF16),
            pltpu.SMEM((NB, R), I32),
            pltpu.VMEM((NB, R), I32),
            pltpu.VMEM((1, R), I32),
            pltpu.VMEM((5, 8, B), F32),
            pltpu.VMEM((R, B, 2 * B), BF16),
            pltpu.VMEM((R, K, B), jnp.int16),
            pltpu.VMEM((N_GRP, SLOTS, K, B), jnp.int16),
            pltpu.VMEM((B, B), F32),
            pltpu.VMEM((N_GRP, SLOTS, B), F32),
            pltpu.VMEM((8, B), I32),
            pltpu.SMEM((8, B), I32),
            dma((4,)),
            dma((7,)),
            dma((4,)),
            dma((4,)),
            dma((4,)),
            dma((4,)),
            dma((N_GRP,)),
            dma((N_GRP,)),
            dma((N_GRP,)),
            dma((N_GRP,)),
        ],
        compiler_params=pltpu.CompilerParams(
            collective_id=0, has_side_effects=True, vmem_limit_bytes=40 << 20
        ),
        name="products",
    )(col_index.T, agg_of_block.reshape(1, R), q_blocks, p_blocks)
    coarse, product = pl.pallas_call(
        coarse_kernel,
        in_specs=[vmem, vmem, any_],
        out_specs=[vmem, any_],
        out_shape=[
            jax.ShapeDtypeStruct((OWN, K, CH * B), F32),
            jax.ShapeDtypeStruct((R, K, B), F32),
        ],
        scratch_shapes=[pltpu.VMEM((CH, K, B), F32)] * OWN
        + [pltpu.VMEM((K, B), I32), pltpu.SMEM((K, B), I32), pltpu.SMEM((OWN, B), I32), pltpu.SMEM((OWN,), I32)]
        + [dma((2,))],
        compiler_params=pltpu.CompilerParams(vmem_limit_bytes=16 << 20),
        name="coarse",
    )(meta_in.reshape(N_GRP * SLOTS, B), w_in.reshape(N_GRP * SLOTS, K, B), prod)
    return product, coarse


def solution(mesh):
    placed = (
        P(("base", "grp"), None, None, None),
        P(("base", "grp"), None, None),
        P(("base", "grp"), None),
        P(("base", "grp"), None),
    )
    return jax.shard_map(
        on_device,
        mesh=mesh,
        in_specs=placed,
        out_specs=(P(("base", "grp"), None, None), P(("base", "grp"), None, None)),
        check_vma=False,
    )
```

```python
import functools

import jax
import jax.numpy as jnp
from jax import lax
from jax.experimental import pallas as pl
from jax.experimental.pallas import tpu as pltpu
from jax.sharding import PartitionSpec as P

F32, BF16, I32 = jnp.float32, jnp.bfloat16, jnp.int32
MESH = pl.DeviceIdType.MESH
R, NB, NB_IN, K, B = 64, 8, 6, 16, 128
N_BASE, N_GRP = 8, 16
OWN = 4
SLOTS = 2 * OWN
STEPS = 32000.0
CH = 24
PAIRS = ((6, 7), (0, 1), (2, 3), (4, 5))


def dot_t(a, b):
    return lax.dot_general(a, b, (((1,), (1,)), ((), ())), preferred_element_type=F32)


def iota(shape, dim):
    return lax.broadcasted_iota(I32, shape, dim)


def product_kernel(
    col_hbm, agg_hbm, q_hbm, p_hbm,
    prod, w_in, meta_in,
    q_v, near, side, col_s, col_v, agg_v, aggtab, split, w_v, pack, info, meta, order_v, order_s,
    q_sem, loc_sem, p_send, p_recv, a_send, a_recv, w_send, w_recv, m_send, m_recv,
):
    base, grp = lax.axis_index("base"), lax.axis_index("grp")
    barrier = pltpu.get_barrier_semaphore()
    for d in range(1, N_GRP):
        pl.semaphore_signal(barrier, 1, device_id={"grp": (grp + d) % N_GRP}, device_id_type=MESH)
    for d in (1, N_BASE - 1):
        pl.semaphore_signal(barrier, 1, device_id={"base": (base + d) % N_BASE}, device_id_type=MESH)
    sends = (
        ({"grp": (grp + 1) % N_GRP}, near, 0, 0),
        ({"grp": (grp + N_GRP - 1) % N_GRP}, near, 2, 2),
        ({"base": (base + 1) % N_BASE}, side, 0, 3),
        ({"base": (base + N_BASE - 1) % N_BASE}, side, 1, 4),
    )
    agg_copy = pltpu.make_async_copy(agg_hbm, agg_v, loc_sem.at[0])
    col_copies = (
        pltpu.make_async_copy(col_hbm, col_s, loc_sem.at[1]),
        pltpu.make_async_copy(col_hbm, col_v, loc_sem.at[2]),
    )
    own_copy = pltpu.make_async_copy(p_hbm, near.at[pl.ds(R, R)], loc_sem.at[3])
    for c in (agg_copy, *col_copies, own_copy):
        c.start()
    q_copies = [
        pltpu.make_async_copy(q_hbm.at[:, pl.ds(a, 2)], q_v.at[:, pl.ds(a, 2)], q_sem.at[c])
        for c, (a, _) in enumerate(PAIRS)
    ]
    for c in q_copies:
        c.start()

    row, lane = iota((R, B), 0), iota((R, B), 1)
    agg_copy.wait()
    agg_row = jnp.concatenate([agg_v[...], jnp.zeros((1, B - R), I32)], 1).astype(F32)
    aggtab[1] = jnp.broadcast_to(agg_row, (8, B))

    pl.semaphore_wait(barrier, N_GRP + 1)
    p_copies, a_copies = [], []
    for s, (to, tab, part, seg) in enumerate(sends):
        p_copies.append(
            pltpu.make_async_remote_copy(
                p_hbm, tab.at[pl.ds(part * R, R)], p_send.at[s], p_recv.at[s], device_id=to, device_id_type=MESH
            )
        )
        a_copies.append(
            pltpu.make_async_remote_copy(
                aggtab.at[1], aggtab.at[seg], a_send.at[s], a_recv.at[s], device_id=to, device_id_type=MESH
            )
        )
    for c in a_copies + p_copies:
        c.start()

    agg_col = jnp.sum(jnp.where(row == lane, agg_row, 0.0), axis=1, keepdims=True)
    before = (agg_col == agg_row) & (lane < row)
    rank = jnp.sum(jnp.where(before, 1.0, 0.0), axis=1, keepdims=True)
    match = (2.0 * agg_col + rank) == lane.astype(F32)
    order = jnp.sum(jnp.where(match, row.astype(F32), 0.0), axis=0, keepdims=True)
    order_v[...] = jnp.broadcast_to(order, (8, B)).astype(I32)
    order_copy = pltpu.make_async_copy(order_v, order_s, loc_sem.at[4])
    order_copy.start()

    def position(c, slot):
        if slot >= NB_IN:
            return (c >> 11) * R + (c & (R - 1))
        shard = jnp.minimum(((c >> 6) - grp + 1) & (N_GRP - 1), 2)
        return shard * R + (c & (R - 1))

    def values(pair, i):
        a, b = pair
        tab = side if a >= NB_IN else near
        zero = jnp.zeros((K, B), BF16)
        left, right = [], []
        for d in range(2):
            left += [tab[position(col_s[a, i + d], a)], zero]
            right += [zero, tab[position(col_s[b, i + d], b)]]
        lhs = jnp.concatenate([jnp.concatenate(left, 0), jnp.concatenate(right, 0)], 1)
        rhs = jnp.concatenate([jnp.concatenate([q_v[i + d, a], q_v[i + d, b]], 1) for d in range(2)], 0)
        out = dot_t(lhs, rhs)
        sums = []
        for d in range(2):
            v = out[2 * d * K : 2 * (d + 1) * K, d * B : (d + 1) * B]
            high = v.astype(BF16)
            split[i + d, a * K : (a + 2) * K, :B] = high
            split[i + d, a * K : (a + 2) * K, B:] = (v - high.astype(F32)).astype(BF16)
            sums.append(v[:K] + v[K:])
        return sums

    for c in col_copies:
        c.wait()
    for c in a_copies:
        c.wait_recv()
    col = jnp.concatenate([col_v[...], jnp.zeros((NB, B - R), I32)], 1)
    near_at, side_at = position(col, 0), position(col, NB_IN)

    def looked_up(low, high, at):
        table = jnp.concatenate([aggtab[low][:, :R], aggtab[high][:, :R]], 1)
        return jnp.take_along_axis(table, at, axis=1)

    inner = jnp.where(near_at < B, looked_up(0, 1, near_at & (B - 1)), looked_up(2, 2, near_at & (B - 1)))
    outer = looked_up(3, 4, side_at & (B - 1))
    colagg = jnp.where(iota((NB, B), 0) < NB_IN, inner, outer) + ((col >> 10) * R).astype(F32)
    info[...] = jnp.zeros_like(info)
    info[:NB] = colagg
    info[NB : NB + 1] = jnp.ones((1, B), F32)

    own_copy.wait()
    for s in (2, 3):
        p_copies[s].wait_recv()
    q_copies[0].wait()

    @pl.loop(0, R // 16)
    def _(j):
        for u in range(0, 16, 2):
            i = j * 16 + u
            for d, v in enumerate(values(PAIRS[0], i)):
                prod[i + d] = v

    for s in (0, 1):
        p_copies[s].wait_recv()
    for c in q_copies[1:]:
        c.wait()

    @pl.loop(0, R // 16)
    def _(j):
        for u in range(0, 16, 2):
            i = j * 16 + u
            all_sums = [values(pair, i) for pair in PAIRS[1:]]
            for d in range(2):
                prod[i + d] += all_sums[0][d] + all_sums[1][d] + all_sums[2][d]

    spot = iota((K, B), 1)

    @pl.loop(0, R // 16)
    def _(j):
        widths = info[K : 2 * K]
        for u in range(0, 16, 2):
            i = j * 16 + u
            p_two = near[pl.ds(R + i, 2)].reshape(2 * K, B)
            out = dot_t(jnp.concatenate([p_two, p_two], 1), split[pl.ds(i, 2)].reshape(2 * B, 2 * B))
            for d in range(2):
                w = out[d * K : (d + 1) * K, d * B : (d + 1) * B]
                most = jnp.max(jnp.abs(w), axis=1, keepdims=True)
                width = jnp.maximum(1.01 * most, 1e-30).astype(BF16).astype(F32)
                w_v[i + d] = jnp.round(w * (STEPS / width)).astype(I32).astype(jnp.int16)
                widths = jnp.where(spot == i + d, width, widths)
        info[K : 2 * K] = widths

    meta[...] = lax.dot_general(
        jnp.where(match, 1.0, 0.0).astype(BF16), info[:, :R].astype(BF16), (((0,), (1,)), ((), ())),
        preferred_element_type=F32,
    ).reshape(N_GRP, SLOTS, B)
    order_copy.wait()

    def gathered(d, to):
        for t in range(SLOTS):
            pack[d, t] = w_v[order_s[0, to * SLOTS + t] & (R - 1)]

    copies = []
    for d in range(1, N_GRP):
        to = (grp + d) % N_GRP
        gathered(d, to)
        for src, dst, send, recv in (
            (pack.at[d], w_in.at[grp], w_send, w_recv),
            (meta.at[to], meta_in.at[grp], m_send, m_recv),
        ):
            copies.append(
                pltpu.make_async_remote_copy(
                    src, dst, send.at[d], recv.at[d], device_id={"grp": to}, device_id_type=MESH
                )
            )
            copies[-1].start()
    gathered(0, grp)
    w_own = pltpu.make_async_copy(pack.at[0], w_in.at[grp], loc_sem.at[5])
    m_own = pltpu.make_async_copy(meta.at[grp], meta_in.at[grp], loc_sem.at[6])
    w_own.start()
    m_own.start()
    for c in p_copies + a_copies:
        c.wait_send()
    w_own.wait()
    m_own.wait()
    for c in copies:
        c.wait()


def coarse_kernel(
    meta, w, prod_in, coarse, prod_out, acc0, acc1, acc2, acc3, rows, chunk_v, turn_v, chunk, turn, sem
):
    copy = pltpu.make_async_copy(prod_in, prod_out, sem.at[0])
    copy.start()
    accs = (acc0, acc1, acc2, acc3)
    turned = meta[...].T
    taken = turned[NB : NB + 1] > 0.5
    col = jnp.where(taken, turned[:NB], 0.0).astype(I32)
    chunk_v[...] = col >> 3
    turn_v[...] = (((col & 7) - iota((NB, B), 0)) & 7) * K
    place_copies = [
        pltpu.make_async_copy(src, dst, sem.at[s]) for src, dst, s in ((chunk_v, chunk, 1), (turn_v, turn, 2))
    ]
    for c in place_copies:
        c.start()
    for acc in accs:
        acc[...] = jnp.zeros_like(acc)
    widths = jnp.where(taken, turned[K : 2 * K] * (1.0 / STEPS), 0.0)
    for e in range(B):
        rows[e] = w[e].astype(I32).astype(F32) * widths[:, e : e + 1]
    for c in place_copies:
        c.wait()

    group = iota((K, B), 1) >> 4

    @pl.loop(0, N_GRP // 4)
    def _(j):
        for u in range(4):
            for t in range(2):
                for n in range(NB):
                    for a, acc in enumerate(accs):
                        e = j * (4 * SLOTS) + (u * SLOTS + 2 * a + t)
                        one = jnp.where(group == n, rows[e], 0.0)
                        acc[chunk[n, e]] += pltpu.roll(one, turn[n, e], 1)

    for a, acc in enumerate(accs):
        for h in range(CH):
            coarse[a, :, h * B : (h + 1) * B] = acc[h]
    copy.wait()


def on_device(q_blocks, p_blocks, col_index, agg_of_block):
    vmem, hbm, any_ = (pl.BlockSpec(memory_space=m) for m in (pltpu.VMEM, pltpu.HBM, pl.ANY))
    dma = pltpu.SemaphoreType.DMA
    inputs = (col_index.T, agg_of_block.reshape(1, R), q_blocks, p_blocks)
    prod, w_in, meta_in = pl.pallas_call(
        product_kernel,
        in_specs=[hbm] * 4,
        out_specs=[vmem, any_, any_],
        out_shape=[
            jax.ShapeDtypeStruct((R, K, B), F32),
            jax.ShapeDtypeStruct((N_GRP, SLOTS, K, B), jnp.int16),
            jax.ShapeDtypeStruct((N_GRP, SLOTS, B), F32),
        ],
        scratch_shapes=[
            pltpu.VMEM((R, NB, B, B), BF16),
            pltpu.VMEM((3 * R, K, B), BF16),
            pltpu.VMEM((2 * R, K, B), BF16),
            pltpu.SMEM((NB, R), I32),
            pltpu.VMEM((NB, R), I32),
            pltpu.VMEM((1, R), I32),
            pltpu.VMEM((5, 8, B), F32),
            pltpu.VMEM((R, B, 2 * B), BF16),
            pltpu.VMEM((R, K, B), jnp.int16),
            pltpu.VMEM((N_GRP, SLOTS, K, B), jnp.int16),
            pltpu.VMEM((B, B), F32),
            pltpu.VMEM((N_GRP, SLOTS, B), F32),
            pltpu.VMEM((8, B), I32),
            pltpu.SMEM((8, B), I32),
            dma((4,)),
            dma((7,)),
            dma((4,)),
            dma((4,)),
            dma((4,)),
            dma((4,)),
            dma((N_GRP,)),
            dma((N_GRP,)),
            dma((N_GRP,)),
            dma((N_GRP,)),
        ],
        compiler_params=pltpu.CompilerParams(
            collective_id=0, has_side_effects=True, vmem_limit_bytes=40 << 20
        ),
        name="products",
    )(*(pltpu.with_memory_space_constraint(x, pltpu.HBM) for x in inputs))
    coarse, product = pl.pallas_call(
        coarse_kernel,
        in_specs=[vmem, vmem, any_],
        out_specs=[vmem, any_],
        out_shape=[
            jax.ShapeDtypeStruct((OWN, K, CH * B), F32),
            jax.ShapeDtypeStruct((R, K, B), F32),
        ],
        scratch_shapes=[pltpu.VMEM((CH, K, B), F32)] * OWN
        + [pltpu.VMEM((B, K, B), F32)]
        + [pltpu.VMEM((NB, B), I32)] * 2
        + [pltpu.SMEM((NB, B), I32)] * 2
        + [dma((3,))],
        compiler_params=pltpu.CompilerParams(vmem_limit_bytes=16 << 20),
        name="coarse",
    )(meta_in.reshape(N_GRP * SLOTS, B), w_in.reshape(N_GRP * SLOTS, K, B), prod)
    return product, coarse


def solution(mesh):
    placed = (
        P(("base", "grp"), None, None, None),
        P(("base", "grp"), None, None),
        P(("base", "grp"), None),
        P(("base", "grp"), None),
    )
    return jax.shard_map(
        on_device,
        mesh=mesh,
        in_specs=placed,
        out_specs=(P(("base", "grp"), None, None), P(("base", "grp"), None, None)),
        check_vma=False,
    )
```

```python
import functools

import jax
import jax.numpy as jnp
from jax import lax
from jax.experimental import pallas as pl
from jax.experimental.pallas import tpu as pltpu
from jax.sharding import PartitionSpec as P

F32, BF16, I32 = jnp.float32, jnp.bfloat16, jnp.int32
MESH = pl.DeviceIdType.MESH
R, NB, NB_IN, K, B = 64, 8, 6, 16, 128
N_BASE, N_GRP = 8, 16
OWN = 4
SLOTS = 2 * OWN
STEPS = 32000.0
CH = 24
SIDE = 4
STEPS_TO = sorted(
    ((dy, dx) for dy in range(SIDE) for dx in range(SIDE)),
    key=lambda d: (-min(d[0], SIDE - d[0]) - min(d[1], SIDE - d[1]), d),
)[:-1]
EARLY, LATE = ((0,),), ((1, 2), (3, 4), (6, 7), (5,))


def dot_t(a, b):
    return lax.dot_general(a, b, (((1,), (1,)), ((), ())), preferred_element_type=F32)


def iota(shape, dim):
    return lax.broadcasted_iota(I32, shape, dim)


def product_kernel(
    col_hbm, agg_hbm, q_hbm, p_hbm,
    prod, w_in,
    q_v, near, side, col_s, col_v, agg_v, aggtab, split, w_v, pack, info, order_v, order_s,
    q_sem, loc_sem, p_send, p_recv, a_send, a_recv, w_send, w_recv,
):
    base, grp = lax.axis_index("base"), lax.axis_index("grp")
    barrier = pltpu.get_barrier_semaphore()
    for d in range(1, N_GRP):
        pl.semaphore_signal(barrier, 1, device_id={"grp": (grp + d) % N_GRP}, device_id_type=MESH)
    for d in (1, N_BASE - 1):
        pl.semaphore_signal(barrier, 1, device_id={"base": (base + d) % N_BASE}, device_id_type=MESH)
    sends = (
        ({"grp": (grp + 1) % N_GRP}, near, 0, 0),
        ({"grp": (grp + N_GRP - 1) % N_GRP}, near, 2, 2),
        ({"base": (base + 1) % N_BASE}, side, 0, 3),
        ({"base": (base + N_BASE - 1) % N_BASE}, side, 1, 4),
    )
    agg_copy = pltpu.make_async_copy(agg_hbm, agg_v, loc_sem.at[0])
    col_copies = (
        pltpu.make_async_copy(col_hbm, col_s, loc_sem.at[1]),
        pltpu.make_async_copy(col_hbm, col_v, loc_sem.at[2]),
    )
    own_copy = pltpu.make_async_copy(p_hbm, near.at[pl.ds(R, R)], loc_sem.at[3])
    for c in (agg_copy, *col_copies, own_copy):
        c.start()
    q_copies = [
        pltpu.make_async_copy(q_hbm.at[:, pl.ds(a, size)], q_v.at[:, pl.ds(a, size)], q_sem.at[c])
        for c, (a, size) in enumerate(((0, 1), (1, 5), (6, 2)))
    ]
    for c in q_copies[:1]:
        c.start()

    row, lane = iota((R, B), 0), iota((R, B), 1)
    agg_copy.wait()
    agg_row = jnp.concatenate([agg_v[...], jnp.zeros((1, B - R), I32)], 1).astype(F32)
    aggtab[1] = jnp.broadcast_to(agg_row, (8, B))

    pl.semaphore_wait(barrier, N_GRP + 1)
    p_copies, a_copies = [], []
    for s, (to, tab, part, seg) in enumerate(sends):
        p_copies.append(
            pltpu.make_async_remote_copy(
                p_hbm, tab.at[pl.ds(part * R, R)], p_send.at[s], p_recv.at[s], device_id=to, device_id_type=MESH
            )
        )
        a_copies.append(
            pltpu.make_async_remote_copy(
                aggtab.at[1], aggtab.at[seg], a_send.at[s], a_recv.at[s], device_id=to, device_id_type=MESH
            )
        )
    for c in a_copies + p_copies:
        c.start()
    for c in q_copies[1:]:
        c.start()

    agg_col = jnp.sum(jnp.where(row == lane, agg_row, 0.0), axis=1, keepdims=True)
    before = (agg_col == agg_row) & (lane < row)
    rank = jnp.sum(jnp.where(before, 1.0, 0.0), axis=1, keepdims=True)
    match = (2.0 * agg_col + rank) == lane.astype(F32)
    order = jnp.sum(jnp.where(match, row.astype(F32), 0.0), axis=0, keepdims=True)
    order_v[...] = jnp.broadcast_to(order, (8, B)).astype(I32)
    order_copy = pltpu.make_async_copy(order_v, order_s, loc_sem.at[4])
    order_copy.start()

    def position(c, slot):
        if slot >= NB_IN:
            return (c >> 11) * R + (c & (R - 1))
        shard = jnp.minimum(((c >> 6) - grp + 1) & (N_GRP - 1), 2)
        return shard * R + (c & (R - 1))

    def block_of(i, n):
        if n == 0:
            return near[R + i]
        return (side if n >= NB_IN else near)[position(col_s[n, i], n)]

    def values(blocks):
        zero = jnp.zeros((K, B), BF16)
        rows = [block_of(*b) for b in blocks]
        lhs = jnp.concatenate(
            [jnp.concatenate([x, zero] if e % 2 == 0 else [zero, x], 1) for e, x in enumerate(rows)], 0
        )
        rhs = jnp.concatenate([jnp.concatenate([q_v[b] for b in blocks[e : e + 2]], 1) for e in (0, 2)], 0)
        out = dot_t(lhs, rhs)
        parts = []
        for e, (i, n) in enumerate(blocks):
            v = out[e * K : (e + 1) * K, e // 2 * B : (e // 2 + 1) * B]
            high = v.astype(BF16)
            split[i, n * K : (n + 1) * K, :B] = high
            split[i, n * K : (n + 1) * K, B:] = (v - high.astype(F32)).astype(BF16)
            parts.append(v)
        return parts

    def four_rows(i, slots):
        sums = [[], [], [], []]
        for group in slots:
            if len(group) == 1:
                sets = [[(d, group[0]) for d in range(4)]]
            else:
                sets = [[(d + e, n) for e in range(2) for n in group] for d in (0, 2)]
            for blocks in sets:
                for (d, _), v in zip(blocks, values([(i + d, n) for d, n in blocks])):
                    sums[d].append(v)
        return [functools.reduce(jnp.add, parts) for parts in sums]

    for c in col_copies:
        c.wait()
    for c in a_copies:
        c.wait_recv()
    col = jnp.concatenate([col_v[...], jnp.zeros((NB, B - R), I32)], 1)
    near_at, side_at = position(col, 0), position(col, NB_IN)

    def looked_up(low, high, at):
        table = jnp.concatenate([aggtab[low][:, :R], aggtab[high][:, :R]], 1)
        return jnp.take_along_axis(table, at, axis=1)

    inner = jnp.where(near_at < B, looked_up(0, 1, near_at & (B - 1)), looked_up(2, 2, near_at & (B - 1)))
    outer = looked_up(3, 4, side_at & (B - 1))
    colagg = jnp.where(iota((NB, B), 0) < NB_IN, inner, outer) + ((col >> 10) * R).astype(F32)
    ones = jnp.where(iota((K - NB, B), 0) == 0, 1.0, 0.0)
    by_row = jnp.concatenate([colagg, ones], 0).astype(BF16)
    info[...] = jnp.dot(by_row[:, :R], jnp.where(match, 1.0, 0.0).astype(BF16), preferred_element_type=F32)

    own_copy.wait()
    q_copies[0].wait()

    @pl.loop(0, R // 16)
    def _(j):
        for u in range(0, 16, 4):
            i = j * 16 + u
            for d, v in enumerate(four_rows(i, EARLY)):
                prod[i + d] = v

    for c in p_copies:
        c.wait_recv()
    for c in q_copies[1:]:
        c.wait()

    @pl.loop(0, R // 16)
    def _(j):
        for u in range(0, 16, 4):
            i = j * 16 + u
            for d, v in enumerate(four_rows(i, LATE)):
                prod[i + d] += v

    order_copy.wait()

    def weights(to, half):
        for t in range(0, SLOTS, 2):
            two = [order_s[0, to * SLOTS + t + d] & (R - 1) for d in range(2)]
            p_two = jnp.concatenate([near[R + i] for i in two], 0)
            out = dot_t(jnp.concatenate([p_two, p_two], 1), jnp.concatenate([split[i] for i in two], 0))
            w_v[half, t] = out[:K, :B]
            w_v[half, t + 1] = out[K:, B:]

    def coded(to, half):
        tile = pltpu.roll(info[...], (B + SLOTS - SLOTS * to) % B, 1)
        for t in range(SLOTS):
            w = w_v[half, t]
            most = jnp.maximum(jnp.max(jnp.abs(w), axis=1, keepdims=True), 1e-30)
            width = jnp.ceil(2.0 * jnp.log2(most) + 0.02)
            pack[to, t] = jnp.round(w * (STEPS / jnp.exp2(0.5 * width))).astype(I32).astype(jnp.int16)
            tile = jnp.where(spot == t, width, tile)
        pack[to, SLOTS] = tile.astype(I32).astype(jnp.int16)

    spot = iota((K, B), 1)
    y, x = grp // SIDE, grp % SIDE
    owners = [(y + dy) % SIDE * SIDE + (x + dx) % SIDE for dy, dx in STEPS_TO] + [grp]
    copies = []
    weights(owners[0], 0)
    for s, to in enumerate(owners):
        if s + 1 < N_GRP:
            weights(owners[s + 1], (s + 1) % 2)
        coded(to, s % 2)
        if s + 1 < N_GRP:
            copies.append(
                pltpu.make_async_remote_copy(
                    pack.at[to], w_in.at[grp], w_send.at[s], w_recv.at[s], device_id={"grp": to}, device_id_type=MESH
                )
            )
        else:
            copies.append(pltpu.make_async_copy(pack.at[to], w_in.at[grp], loc_sem.at[5]))
        copies[-1].start()
    for c in p_copies + a_copies:
        c.wait_send()
    for c in copies:
        c.wait()


def coarse_kernel(
    w, prod_in, coarse, prod_out, acc0, acc1, acc2, acc3, rows, chunk_v, turn_v, chunk, turn, sem
):
    copy = pltpu.make_async_copy(prod_in, prod_out, sem.at[0])
    copy.start()
    accs = (acc0, acc1, acc2, acc3)
    owner_of = iota((K, B), 1) // SLOTS
    widths, cols = jnp.zeros((K, B), F32), jnp.zeros((K, B), F32)
    for src in range(N_GRP):
        tile = w[src, SLOTS].astype(I32).astype(F32)
        widths = jnp.where(owner_of == src, pltpu.roll(tile, src * SLOTS, 1), widths)
        cols = jnp.where(owner_of == src, pltpu.roll(tile, (src + N_GRP - 1) % N_GRP * SLOTS, 1), cols)
    taken = cols[NB : NB + 1] > 0.5
    col = jnp.where(taken, cols[:NB], 0.0).astype(I32)
    chunk_v[...] = col >> 3
    turn_v[...] = (((col & 7) - iota((NB, B), 0)) & 7) * K
    place_copies = [
        pltpu.make_async_copy(src, dst, sem.at[s]) for src, dst, s in ((chunk_v, chunk, 1), (turn_v, turn, 2))
    ]
    for c in place_copies:
        c.start()
    for acc in accs:
        acc[...] = jnp.zeros_like(acc)
    widths = jnp.where(taken, jnp.exp2(0.5 * widths) * (1.0 / STEPS), 0.0)
    for e in range(B):
        rows[e] = w[e // SLOTS, e % SLOTS].astype(I32).astype(F32) * widths[:, e : e + 1]
    for c in place_copies:
        c.wait()

    group = iota((K, B), 1) >> 4

    @pl.loop(0, N_GRP // 4)
    def _(j):
        for u in range(4):
            for t in range(2):
                for n in range(NB):
                    for a, acc in enumerate(accs):
                        e = j * (4 * SLOTS) + (u * SLOTS + 2 * a + t)
                        one = jnp.where(group == n, rows[e], 0.0)
                        acc[chunk[n, e]] += pltpu.roll(one, turn[n, e], 1)

    for a, acc in enumerate(accs):
        for h in range(CH):
            coarse[a, :, h * B : (h + 1) * B] = acc[h]
    copy.wait()


def on_device(q_blocks, p_blocks, col_index, agg_of_block):
    vmem, hbm, any_ = (pl.BlockSpec(memory_space=m) for m in (pltpu.VMEM, pltpu.HBM, pl.ANY))
    dma = pltpu.SemaphoreType.DMA
    inputs = (col_index.T, agg_of_block.reshape(1, R), q_blocks, p_blocks)
    prod, w_in = pl.pallas_call(
        product_kernel,
        in_specs=[hbm] * 4,
        out_specs=[vmem, any_],
        out_shape=[
            jax.ShapeDtypeStruct((R, K, B), F32),
            jax.ShapeDtypeStruct((N_GRP, SLOTS + 1, K, B), jnp.int16),
        ],
        scratch_shapes=[
            pltpu.VMEM((R, NB, B, B), BF16),
            pltpu.VMEM((3 * R, K, B), BF16),
            pltpu.VMEM((2 * R, K, B), BF16),
            pltpu.SMEM((NB, R), I32),
            pltpu.VMEM((NB, R), I32),
            pltpu.VMEM((1, R), I32),
            pltpu.VMEM((5, 8, B), F32),
            pltpu.VMEM((R, B, 2 * B), BF16),
            pltpu.VMEM((2, SLOTS, K, B), F32),
            pltpu.VMEM((N_GRP, SLOTS + 1, K, B), jnp.int16),
            pltpu.VMEM((K, B), F32),
            pltpu.VMEM((8, B), I32),
            pltpu.SMEM((8, B), I32),
            dma((3,)),
            dma((6,)),
            dma((4,)),
            dma((4,)),
            dma((4,)),
            dma((4,)),
            dma((N_GRP,)),
            dma((N_GRP,)),
        ],
        compiler_params=pltpu.CompilerParams(
            collective_id=0, has_side_effects=True, vmem_limit_bytes=40 << 20
        ),
        name="products",
    )(*(pltpu.with_memory_space_constraint(x, pltpu.HBM) for x in inputs))
    coarse, product = pl.pallas_call(
        coarse_kernel,
        in_specs=[vmem, any_],
        out_specs=[vmem, any_],
        out_shape=[
            jax.ShapeDtypeStruct((OWN, K, CH * B), F32),
            jax.ShapeDtypeStruct((R, K, B), F32),
        ],
        scratch_shapes=[pltpu.VMEM((CH, K, B), F32)] * OWN
        + [pltpu.VMEM((B, K, B), F32)]
        + [pltpu.VMEM((NB, B), I32)] * 2
        + [pltpu.SMEM((NB, B), I32)] * 2
        + [dma((3,))],
        compiler_params=pltpu.CompilerParams(vmem_limit_bytes=16 << 20),
        name="coarse",
    )(w_in, prod)
    return product, coarse


def solution(mesh):
    placed = (
        P(("base", "grp"), None, None, None),
        P(("base", "grp"), None, None),
        P(("base", "grp"), None),
        P(("base", "grp"), None),
    )
    return jax.shard_map(
        on_device,
        mesh=mesh,
        in_specs=placed,
        out_specs=(P(("base", "grp"), None, None), P(("base", "grp"), None, None)),
        check_vma=False,
    )
```

```python
import functools

import jax
import jax.numpy as jnp
from jax import lax
from jax.experimental import pallas as pl
from jax.experimental.pallas import tpu as pltpu
from jax.sharding import PartitionSpec as P

F32, BF16, I32 = jnp.float32, jnp.bfloat16, jnp.int32
MESH = pl.DeviceIdType.MESH
R, NB, NB_IN, K, B = 64, 8, 6, 16, 128
N_BASE, N_GRP = 8, 16
OWN = 4
SLOTS = 2 * OWN
STEPS = 32000.0
CH = 24
SIDE = 4
STEPS_TO = sorted(
    ((dy, dx) for dy in range(SIDE) for dx in range(SIDE)),
    key=lambda d: (-min(d[0], SIDE - d[0]) - min(d[1], SIDE - d[1]), d),
)[:-1]
EARLY, LATE = ((0,),), ((1, 2), (3, 4), (6, 7), (5,))


def dot_t(a, b):
    return lax.dot_general(a, b, (((1,), (1,)), ((), ())), preferred_element_type=F32)


def iota(shape, dim):
    return lax.broadcasted_iota(I32, shape, dim)


def product_kernel(
    col_hbm, agg_hbm, q_hbm, p_hbm,
    prod, w_in,
    q_v, near, side, col_s, col_v, agg_v, aggtab, split, w_v, pack, info, order_v, order_s, first, prod_v,
    q_sem, loc_sem, p_send, p_recv, a_send, a_recv, w_send, w_recv,
):
    base, grp = lax.axis_index("base"), lax.axis_index("grp")
    barrier = pltpu.get_barrier_semaphore()
    for d in range(1, N_GRP):
        pl.semaphore_signal(barrier, 1, device_id={"grp": (grp + d) % N_GRP}, device_id_type=MESH)
    for d in (1, N_BASE - 1):
        pl.semaphore_signal(barrier, 1, device_id={"base": (base + d) % N_BASE}, device_id_type=MESH)
    sends = (
        ({"grp": (grp + 1) % N_GRP}, near, 0, 0),
        ({"grp": (grp + N_GRP - 1) % N_GRP}, near, 2, 2),
        ({"base": (base + 1) % N_BASE}, side, 0, 3),
        ({"base": (base + N_BASE - 1) % N_BASE}, side, 1, 4),
    )
    agg_copy = pltpu.make_async_copy(agg_hbm, agg_v, loc_sem.at[0])
    col_copies = (
        pltpu.make_async_copy(col_hbm, col_s, loc_sem.at[1]),
        pltpu.make_async_copy(col_hbm, col_v, loc_sem.at[2]),
    )
    own_copy = pltpu.make_async_copy(p_hbm, near.at[pl.ds(R, R)], loc_sem.at[3])
    for c in (agg_copy, *col_copies, own_copy):
        c.start()
    q_copies = [
        pltpu.make_async_copy(q_hbm.at[:, pl.ds(a, size)], q_v.at[:, pl.ds(a, size)], q_sem.at[c])
        for c, (a, size) in enumerate(((0, 1), (1, 5), (6, 2)))
    ]
    for c in q_copies[:1]:
        c.start()

    row, lane = iota((R, B), 0), iota((R, B), 1)
    agg_copy.wait()
    agg_row = jnp.concatenate([agg_v[...], jnp.zeros((1, B - R), I32)], 1).astype(F32)
    aggtab[1] = jnp.broadcast_to(agg_row, (8, B))

    pl.semaphore_wait(barrier, N_GRP + 1)
    p_copies, a_copies = [], []
    for s, (to, tab, part, seg) in enumerate(sends):
        p_copies.append(
            pltpu.make_async_remote_copy(
                p_hbm, tab.at[pl.ds(part * R, R)], p_send.at[s], p_recv.at[s], device_id=to, device_id_type=MESH
            )
        )
        a_copies.append(
            pltpu.make_async_remote_copy(
                aggtab.at[1], aggtab.at[seg], a_send.at[s], a_recv.at[s], device_id=to, device_id_type=MESH
            )
        )
    for c in a_copies + p_copies:
        c.start()
    for c in q_copies[1:]:
        c.start()

    agg_col = jnp.sum(jnp.where(row == lane, agg_row, 0.0), axis=1, keepdims=True)
    before = (agg_col == agg_row) & (lane < row)
    rank = jnp.sum(jnp.where(before, 1.0, 0.0), axis=1, keepdims=True)
    y, x = grp // SIDE, grp % SIDE
    agg_int = agg_col.astype(I32)
    step = (((agg_int >> 4) - y) & (SIDE - 1)) * SIDE + (((agg_int >> 2) - x) & (SIDE - 1))
    turn = jnp.full((R, 1), 1.0 * len(STEPS_TO), F32)
    for s, (dy, dx) in enumerate(STEPS_TO):
        turn = jnp.where(step == dy * SIDE + dx, 1.0 * s, turn)
    place = SLOTS * turn + 2.0 * (agg_int & (OWN - 1)).astype(F32) + rank

    def across(taken, value):
        return jnp.sum(jnp.where(taken, value, 0.0), axis=0, keepdims=True)

    row_f, lane_f = row.astype(F32), lane.astype(F32)
    match = place == lane_f
    ahead = (across(row == lane, place) < place) & (lane < R)
    position_of = jnp.sum(jnp.where(ahead, 1.0, 0.0), axis=1, keepdims=True)
    lists = [
        across(match, row_f),
        across(match, position_of),
        across(position_of == lane_f, row_f),
        across(row == lane, position_of),
        jnp.zeros((4, B), F32),
    ]
    order_v[...] = jnp.concatenate(lists, 0).astype(I32)
    order_copy = pltpu.make_async_copy(order_v, order_s, loc_sem.at[4])
    order_copy.start()

    def position(c, slot):
        if slot >= NB_IN:
            return (c >> 11) * R + (c & (R - 1))
        shard = jnp.minimum(((c >> 6) - grp + 1) & (N_GRP - 1), 2)
        return shard * R + (c & (R - 1))

    def block_of(i, n):
        if n == 0:
            return near[R + i]
        return (side if n >= NB_IN else near)[position(col_s[n, i], n)]

    def values(blocks):
        zero = jnp.zeros((K, B), BF16)
        rows = [block_of(i, n) for i, n, _ in blocks]
        lhs = jnp.concatenate(
            [jnp.concatenate([v, zero] if e % 2 == 0 else [zero, v], 1) for e, v in enumerate(rows)], 0
        )
        rhs = jnp.concatenate(
            [jnp.concatenate([q_v[i, n] for i, n, _ in blocks[e : e + 2]], 1) for e in (0, 2)], 0
        )
        out = dot_t(lhs, rhs)
        parts = []
        for e, (_, n, at) in enumerate(blocks):
            v = out[e * K : (e + 1) * K, e // 2 * B : (e // 2 + 1) * B]
            high = v.astype(BF16)
            low = (v - high.astype(F32)).astype(BF16)
            if n == 0:
                first[at, :, :B] = high
                first[at, :, B:] = low
            else:
                split[at, (n - 1) * K : n * K, :B] = high
                split[at, (n - 1) * K : n * K, B:] = low
            parts.append(v)
        return parts

    def four_rows(rows, ats, slots):
        sums = [[], [], [], []]
        for group in slots:
            if len(group) == 1:
                sets = [[(d, group[0]) for d in range(4)]]
            else:
                sets = [[(d + e, n) for e in range(2) for n in group] for d in (0, 2)]
            for blocks in sets:
                for (d, _), v in zip(blocks, values([(rows[d], n, ats[d]) for d, n in blocks])):
                    sums[d].append(v)
        return [functools.reduce(jnp.add, parts) for parts in sums]

    for c in col_copies:
        c.wait()
    for c in a_copies:
        c.wait_recv()
    col = jnp.concatenate([col_v[...], jnp.zeros((NB, B - R), I32)], 1)
    near_at, side_at = position(col, 0), position(col, NB_IN)

    def looked_up(low, high, at):
        table = jnp.concatenate([aggtab[low][:, :R], aggtab[high][:, :R]], 1)
        return jnp.take_along_axis(table, at, axis=1)

    inner = jnp.where(near_at < B, looked_up(0, 1, near_at & (B - 1)), looked_up(2, 2, near_at & (B - 1)))
    outer = looked_up(3, 4, side_at & (B - 1))
    colagg = jnp.where(iota((NB, B), 0) < NB_IN, inner, outer) + ((col >> 10) * R).astype(F32)
    ones = jnp.where(iota((K - NB, B), 0) == 0, 1.0, 0.0)
    by_row = jnp.concatenate([colagg, ones], 0).astype(BF16)
    info[...] = jnp.dot(by_row[:, :R], jnp.where(match, 1.0, 0.0).astype(BF16), preferred_element_type=F32)

    own_copy.wait()
    q_copies[0].wait()

    @pl.loop(0, R // 16)
    def _(j):
        for u in range(0, 16, 4):
            i = j * 16 + u
            four = [i + d for d in range(4)]
            for d, v in enumerate(four_rows(four, four, EARLY)):
                prod[i + d] = v

    for c in p_copies:
        c.wait_recv()
    for c in q_copies[1:]:
        c.wait()

    order_copy.wait()

    def late(c):
        for u in range(0, 16, 4):
            ats = [c * 16 + u + d for d in range(4)]
            rows = [order_s[2, at] & (R - 1) for at in ats]
            for at, v in zip(ats, four_rows(rows, ats, LATE)):
                prod_v[at] = v

    def weights(s):
        for t in range(0, SLOTS, 2):
            p_two, v_two = [], []
            for e in (s * SLOTS + t, s * SLOTS + t + 1):
                i = order_s[0, e] & (R - 1)
                p_two.append(near[R + i])
                v_two += [first[i], split[order_s[1, e] & (R - 1)]]
            p_two = jnp.concatenate(p_two, 0)
            out = dot_t(jnp.concatenate([p_two, p_two], 1), jnp.concatenate(v_two, 0))
            w_v[s % 2, t] = out[:K, :B]
            w_v[s % 2, t + 1] = out[K:, B:]

    def coded(s):
        tile = pltpu.roll(info[...], (B + SLOTS - SLOTS * s) % B, 1)
        for t in range(SLOTS):
            w = w_v[s % 2, t]
            most = jnp.maximum(jnp.max(jnp.abs(w), axis=1, keepdims=True), 1e-30)
            width = jnp.ceil(2.0 * jnp.log2(most) + 0.02)
            pack[s, t] = jnp.round(w * (STEPS / jnp.exp2(0.5 * width))).astype(I32).astype(jnp.int16)
            tile = jnp.where(spot == t, width, tile)
        pack[s, SLOTS] = tile.astype(I32).astype(jnp.int16)

    copies = []

    def send(s):
        if s < len(STEPS_TO):
            dy, dx = STEPS_TO[s]
            to = (y + dy) % SIDE * SIDE + (x + dx) % SIDE
            copy = pltpu.make_async_remote_copy(
                pack.at[s], w_in.at[grp], w_send.at[s], w_recv.at[s], device_id={"grp": to}, device_id_type=MESH
            )
        else:
            copy = pltpu.make_async_copy(pack.at[s], w_in.at[grp], loc_sem.at[5])
        copy.start()
        copies.append(copy)

    spot = iota((K, B), 1)
    late(0)
    for c in range(1, R // 16):
        two = (2 * c - 2, 2 * c - 1)
        for s in two:
            weights(s)
        late(c)
        for s in two:
            coded(s)
        for s in two:
            send(s)
    begin = R // 8 - 2
    weights(begin)
    for s in range(begin, N_GRP):
        if s + 1 < N_GRP:
            weights(s + 1)
        coded(s)
        send(s)

    @pl.loop(0, R // 8)
    def _(j):
        for u in range(8):
            i = j * 8 + u
            prod[i] += prod_v[order_s[3, i] & (R - 1)]

    for c in p_copies + a_copies:
        c.wait_send()
    for c in copies:
        c.wait()


def coarse_kernel(
    w, prod_in, coarse, prod_out, acc0, acc1, acc2, acc3, rows, chunk_v, turn_v, chunk, turn, sem
):
    copy = pltpu.make_async_copy(prod_in, prod_out, sem.at[0])
    copy.start()
    accs = (acc0, acc1, acc2, acc3)
    owner_of = iota((K, B), 1) // SLOTS
    widths, cols = jnp.zeros((K, B), F32), jnp.zeros((K, B), F32)
    for src in range(N_GRP):
        tile = w[src, SLOTS].astype(I32).astype(F32)
        widths = jnp.where(owner_of == src, pltpu.roll(tile, src * SLOTS, 1), widths)
        cols = jnp.where(owner_of == src, pltpu.roll(tile, (src + N_GRP - 1) % N_GRP * SLOTS, 1), cols)
    taken = cols[NB : NB + 1] > 0.5
    col = jnp.where(taken, cols[:NB], 0.0).astype(I32)
    chunk_v[...] = col >> 3
    turn_v[...] = (((col & 7) - iota((NB, B), 0)) & 7) * K
    place_copies = [
        pltpu.make_async_copy(src, dst, sem.at[s]) for src, dst, s in ((chunk_v, chunk, 1), (turn_v, turn, 2))
    ]
    for c in place_copies:
        c.start()
    for acc in accs:
        acc[...] = jnp.zeros_like(acc)
    widths = jnp.where(taken, jnp.exp2(0.5 * widths) * (1.0 / STEPS), 0.0)
    for e in range(B):
        rows[e] = w[e // SLOTS, e % SLOTS].astype(I32).astype(F32) * widths[:, e : e + 1]
    for c in place_copies:
        c.wait()

    group = iota((K, B), 1) >> 4

    @pl.loop(0, N_GRP // 4)
    def _(j):
        for u in range(4):
            for t in range(2):
                for n in range(NB):
                    for a, acc in enumerate(accs):
                        e = j * (4 * SLOTS) + (u * SLOTS + 2 * a + t)
                        one = jnp.where(group == n, rows[e], 0.0)
                        acc[chunk[n, e]] += pltpu.roll(one, turn[n, e], 1)

    for a, acc in enumerate(accs):
        for h in range(CH):
            coarse[a, :, h * B : (h + 1) * B] = acc[h]
    copy.wait()


def on_device(q_blocks, p_blocks, col_index, agg_of_block):
    vmem, hbm, any_ = (pl.BlockSpec(memory_space=m) for m in (pltpu.VMEM, pltpu.HBM, pl.ANY))
    dma = pltpu.SemaphoreType.DMA
    inputs = (col_index.T, agg_of_block.reshape(1, R), q_blocks, p_blocks)
    prod, w_in = pl.pallas_call(
        product_kernel,
        in_specs=[hbm] * 4,
        out_specs=[vmem, any_],
        out_shape=[
            jax.ShapeDtypeStruct((R, K, B), F32),
            jax.ShapeDtypeStruct((N_GRP, SLOTS + 1, K, B), jnp.int16),
        ],
        scratch_shapes=[
            pltpu.VMEM((R, NB, B, B), BF16),
            pltpu.VMEM((3 * R, K, B), BF16),
            pltpu.VMEM((2 * R, K, B), BF16),
            pltpu.SMEM((NB, R), I32),
            pltpu.VMEM((NB, R), I32),
            pltpu.VMEM((1, R), I32),
            pltpu.VMEM((5, 8, B), F32),
            pltpu.VMEM((R, (NB - 1) * K, 2 * B), BF16),
            pltpu.VMEM((2, SLOTS, K, B), F32),
            pltpu.VMEM((N_GRP, SLOTS + 1, K, B), jnp.int16),
            pltpu.VMEM((K, B), F32),
            pltpu.VMEM((8, B), I32),
            pltpu.SMEM((8, B), I32),
            pltpu.VMEM((R, K, 2 * B), BF16),
            pltpu.VMEM((R, K, B), F32),
            dma((3,)),
            dma((6,)),
            dma((4,)),
            dma((4,)),
            dma((4,)),
            dma((4,)),
            dma((N_GRP,)),
            dma((N_GRP,)),
        ],
        compiler_params=pltpu.CompilerParams(
            collective_id=0, has_side_effects=True, vmem_limit_bytes=40 << 20
        ),
        name="products",
    )(*(pltpu.with_memory_space_constraint(x, pltpu.HBM) for x in inputs))
    coarse, product = pl.pallas_call(
        coarse_kernel,
        in_specs=[vmem, any_],
        out_specs=[vmem, any_],
        out_shape=[
            jax.ShapeDtypeStruct((OWN, K, CH * B), F32),
            jax.ShapeDtypeStruct((R, K, B), F32),
        ],
        scratch_shapes=[pltpu.VMEM((CH, K, B), F32)] * OWN
        + [pltpu.VMEM((B, K, B), F32)]
        + [pltpu.VMEM((NB, B), I32)] * 2
        + [pltpu.SMEM((NB, B), I32)] * 2
        + [dma((3,))],
        compiler_params=pltpu.CompilerParams(vmem_limit_bytes=16 << 20),
        name="coarse",
    )(w_in, prod)
    return product, coarse


def solution(mesh):
    placed = (
        P(("base", "grp"), None, None, None),
        P(("base", "grp"), None, None),
        P(("base", "grp"), None),
        P(("base", "grp"), None),
    )
    return jax.shard_map(
        on_device,
        mesh=mesh,
        in_specs=placed,
        out_specs=(P(("base", "grp"), None, None), P(("base", "grp"), None, None)),
        check_vma=False,
    )
```

```python
import functools

import jax
import jax.numpy as jnp
from jax import lax
from jax.experimental import pallas as pl
from jax.experimental.pallas import tpu as pltpu
from jax.sharding import PartitionSpec as P

F32, BF16, I32 = jnp.float32, jnp.bfloat16, jnp.int32
MESH = pl.DeviceIdType.MESH
R, NB, NB_IN, K, B = 64, 8, 6, 16, 128
N_BASE, N_GRP = 8, 16
OWN = 4
SLOTS = 2 * OWN
STEPS = 32000.0
CH = 24
SIDE = 4
STEPS_TO = sorted(
    ((dy, dx) for dy in range(SIDE) for dx in range(SIDE)),
    key=lambda d: (-min(d[0], SIDE - d[0]) - min(d[1], SIDE - d[1]), d),
)[:-1]
EARLY, LATE = ((0,),), ((1, 2), (3, 4), (6, 7), (5,))


def dot_t(a, b):
    return lax.dot_general(a, b, (((1,), (1,)), ((), ())), preferred_element_type=F32)


def iota(shape, dim):
    return lax.broadcasted_iota(I32, shape, dim)


def product_kernel(
    col_hbm, agg_hbm, q_hbm, p_hbm,
    prod, w_in,
    q_v, near, side, col_s, col_v, agg_v, aggtab, split, w_v, pack, info, order_v, order_s, first, prod_v,
    q_sem, loc_sem, p_send, p_recv, a_send, a_recv, w_send, w_recv,
):
    base, grp = lax.axis_index("base"), lax.axis_index("grp")
    barrier = pltpu.get_barrier_semaphore()
    for d in range(1, N_GRP):
        pl.semaphore_signal(barrier, 1, device_id={"grp": (grp + d) % N_GRP}, device_id_type=MESH)
    for d in (1, N_BASE - 1):
        pl.semaphore_signal(barrier, 1, device_id={"base": (base + d) % N_BASE}, device_id_type=MESH)
    sends = (
        ({"grp": (grp + 1) % N_GRP}, near, 0, 0),
        ({"grp": (grp + N_GRP - 1) % N_GRP}, near, 2, 2),
        ({"base": (base + 1) % N_BASE}, side, 0, 3),
        ({"base": (base + N_BASE - 1) % N_BASE}, side, 1, 4),
    )
    agg_copy = pltpu.make_async_copy(agg_hbm, agg_v, loc_sem.at[0])
    col_copies = (
        pltpu.make_async_copy(col_hbm, col_s, loc_sem.at[1]),
        pltpu.make_async_copy(col_hbm, col_v, loc_sem.at[2]),
    )
    own_copy = pltpu.make_async_copy(p_hbm, near.at[pl.ds(R, R)], loc_sem.at[3])
    for c in (agg_copy, *col_copies, own_copy):
        c.start()
    q_copies = [
        pltpu.make_async_copy(q_hbm.at[:, pl.ds(a, size)], q_v.at[:, pl.ds(a, size)], q_sem.at[c])
        for c, (a, size) in enumerate(((0, 1), (1, 5), (6, 2)))
    ]
    for c in q_copies[:1]:
        c.start()

    row, lane = iota((R, B), 0), iota((R, B), 1)
    agg_copy.wait()
    agg_row = jnp.concatenate([agg_v[...], jnp.zeros((1, B - R), I32)], 1).astype(F32)
    aggtab[1] = jnp.broadcast_to(agg_row, (8, B))

    pl.semaphore_wait(barrier, N_GRP + 1)
    p_copies, a_copies = [], []
    for s, (to, tab, part, seg) in enumerate(sends):
        p_copies.append(
            pltpu.make_async_remote_copy(
                p_hbm, tab.at[pl.ds(part * R, R)], p_send.at[s], p_recv.at[s], device_id=to, device_id_type=MESH
            )
        )
        a_copies.append(
            pltpu.make_async_remote_copy(
                aggtab.at[1], aggtab.at[seg], a_send.at[s], a_recv.at[s], device_id=to, device_id_type=MESH
            )
        )
    for c in a_copies + p_copies:
        c.start()
    for c in q_copies[1:]:
        c.start()

    agg_col = jnp.sum(jnp.where(row == lane, agg_row, 0.0), axis=1, keepdims=True)
    before = (agg_col == agg_row) & (lane < row)
    rank = jnp.sum(jnp.where(before, 1.0, 0.0), axis=1, keepdims=True)
    y, x = grp // SIDE, grp % SIDE
    agg_int = agg_col.astype(I32)
    step = (((agg_int >> 4) - y) & (SIDE - 1)) * SIDE + (((agg_int >> 2) - x) & (SIDE - 1))
    turn = jnp.full((R, 1), 1.0 * len(STEPS_TO), F32)
    for s, (dy, dx) in enumerate(STEPS_TO):
        turn = jnp.where(step == dy * SIDE + dx, 1.0 * s, turn)
    place = SLOTS * turn + 2.0 * (agg_int & (OWN - 1)).astype(F32) + rank

    def across(taken, value):
        return jnp.sum(jnp.where(taken, value, 0.0), axis=0, keepdims=True)

    row_f, lane_f = row.astype(F32), lane.astype(F32)
    match = place == lane_f
    ahead = (across(row == lane, place) < place) & (lane < R)
    position_of = jnp.sum(jnp.where(ahead, 1.0, 0.0), axis=1, keepdims=True)
    lists = [
        across(match, row_f),
        across(match, position_of),
        across(position_of == lane_f, row_f),
        across(row == lane, position_of),
        jnp.zeros((4, B), F32),
    ]
    order_v[...] = jnp.concatenate(lists, 0).astype(I32)
    order_copy = pltpu.make_async_copy(order_v, order_s, loc_sem.at[4])
    order_copy.start()

    def position(c, slot):
        if slot >= NB_IN:
            return (c >> 11) * R + (c & (R - 1))
        shard = jnp.minimum(((c >> 6) - grp + 1) & (N_GRP - 1), 2)
        return shard * R + (c & (R - 1))

    def block_of(i, n):
        if n == 0:
            return near[R + i]
        return (side if n >= NB_IN else near)[position(col_s[n, i], n)]

    def values(blocks):
        zero = jnp.zeros((K, B), BF16)
        rows = [block_of(i, n) for i, n, _ in blocks]
        lhs = jnp.concatenate(
            [jnp.concatenate([v, zero] if e % 2 == 0 else [zero, v], 1) for e, v in enumerate(rows)], 0
        )
        rhs = jnp.concatenate(
            [jnp.concatenate([q_v[i, n] for i, n, _ in blocks[e : e + 2]], 1) for e in (0, 2)], 0
        )
        out = dot_t(lhs, rhs)
        parts = []
        for e, (_, n, at) in enumerate(blocks):
            v = out[e * K : (e + 1) * K, e // 2 * B : (e // 2 + 1) * B]
            high = v.astype(BF16)
            low = (v - high.astype(F32)).astype(BF16)
            if n == 0:
                first[at, :, :B] = high
                first[at, :, B:] = low
            else:
                split[at, (n - 1) * K : n * K, :B] = high
                split[at, (n - 1) * K : n * K, B:] = low
            parts.append(v)
        return parts

    def four_rows(rows, ats, slots):
        sums = [[], [], [], []]
        for group in slots:
            if len(group) == 1:
                sets = [[(d, group[0]) for d in range(4)]]
            else:
                sets = [[(d + e, n) for e in range(2) for n in group] for d in (0, 2)]
            for blocks in sets:
                for (d, _), v in zip(blocks, values([(rows[d], n, ats[d]) for d, n in blocks])):
                    sums[d].append(v)
        return [functools.reduce(jnp.add, parts) for parts in sums]

    for c in col_copies:
        c.wait()
    for c in a_copies:
        c.wait_recv()
    col = jnp.concatenate([col_v[...], jnp.zeros((NB, B - R), I32)], 1)
    near_at, side_at = position(col, 0), position(col, NB_IN)

    def looked_up(low, high, at):
        table = jnp.concatenate([aggtab[low][:, :R], aggtab[high][:, :R]], 1)
        return jnp.take_along_axis(table, at, axis=1)

    inner = jnp.where(near_at < B, looked_up(0, 1, near_at & (B - 1)), looked_up(2, 2, near_at & (B - 1)))
    outer = looked_up(3, 4, side_at & (B - 1))
    colagg = jnp.where(iota((NB, B), 0) < NB_IN, inner, outer) + ((col >> 10) * R).astype(F32)
    ones = jnp.where(iota((K - NB, B), 0) == 0, 1.0, 0.0)
    by_row = jnp.concatenate([colagg, ones], 0).astype(BF16)
    info[...] = jnp.dot(by_row[:, :R], jnp.where(match, 1.0, 0.0).astype(BF16), preferred_element_type=F32)

    own_copy.wait()
    q_copies[0].wait()

    @pl.loop(0, R // 16)
    def _(j):
        for u in range(0, 16, 4):
            i = j * 16 + u
            four = [i + d for d in range(4)]
            for d, v in enumerate(four_rows(four, four, EARLY)):
                prod[i + d] = v

    for c in p_copies:
        c.wait_recv()
    for c in q_copies[1:]:
        c.wait()

    order_copy.wait()

    def late(c):
        for u in range(0, 8, 4):
            ats = [c * 8 + u + d for d in range(4)]
            rows = [order_s[2, at] & (R - 1) for at in ats]
            for at, v in zip(ats, four_rows(rows, ats, LATE)):
                prod_v[at] = v

    def weights(s):
        for t in range(0, SLOTS, 2):
            p_two, v_two = [], []
            for e in (s * SLOTS + t, s * SLOTS + t + 1):
                i = order_s[0, e] & (R - 1)
                p_two.append(near[R + i])
                v_two += [first[i], split[order_s[1, e] & (R - 1)]]
            p_two = jnp.concatenate(p_two, 0)
            out = dot_t(jnp.concatenate([p_two, p_two], 1), jnp.concatenate(v_two, 0))
            w_v[s % 2, t] = out[:K, :B]
            w_v[s % 2, t + 1] = out[K:, B:]

    def coded(s):
        tile = pltpu.roll(info[...], (B + SLOTS - SLOTS * s) % B, 1)
        for t in range(SLOTS):
            w = w_v[s % 2, t]
            most = jnp.maximum(jnp.max(jnp.abs(w), axis=1, keepdims=True), 1e-30)
            width = jnp.ceil(2.0 * jnp.log2(most) + 0.02)
            pack[s, t] = jnp.round(w * (STEPS / jnp.exp2(0.5 * width))).astype(I32).astype(jnp.int16)
            tile = jnp.where(spot == t, width, tile)
        pack[s, SLOTS] = tile.astype(I32).astype(jnp.int16)

    copies = []

    def send(s):
        if s < len(STEPS_TO):
            dy, dx = STEPS_TO[s]
            to = (y + dy) % SIDE * SIDE + (x + dx) % SIDE
            copy = pltpu.make_async_remote_copy(
                pack.at[s], w_in.at[grp], w_send.at[s], w_recv.at[s], device_id={"grp": to}, device_id_type=MESH
            )
        else:
            copy = pltpu.make_async_copy(pack.at[s], w_in.at[grp], loc_sem.at[5])
        copy.start()
        copies.append(copy)

    spot = iota((K, B), 1)
    late(0)
    for c in range(1, R // 8):
        weights(c - 1)
        late(c)
        coded(c - 1)
        send(c - 1)
    begin = R // 8 - 1
    weights(begin)
    for s in range(begin, N_GRP):
        if s + 1 < N_GRP:
            weights(s + 1)
        coded(s)
        send(s)

    @pl.loop(0, R // 8)
    def _(j):
        for u in range(8):
            i = j * 8 + u
            prod[i] += prod_v[order_s[3, i] & (R - 1)]

    for c in p_copies + a_copies:
        c.wait_send()
    for c in copies:
        c.wait()


def coarse_kernel(
    w, prod_in, coarse, prod_out, acc0, acc1, acc2, acc3, rows, chunk_v, turn_v, chunk, turn, sem
):
    copy = pltpu.make_async_copy(prod_in, prod_out, sem.at[0])
    copy.start()
    accs = (acc0, acc1, acc2, acc3)
    owner_of = iota((K, B), 1) // SLOTS
    widths, cols = jnp.zeros((K, B), F32), jnp.zeros((K, B), F32)
    for src in range(N_GRP):
        tile = w[src, SLOTS].astype(I32).astype(F32)
        widths = jnp.where(owner_of == src, pltpu.roll(tile, src * SLOTS, 1), widths)
        cols = jnp.where(owner_of == src, pltpu.roll(tile, (src + N_GRP - 1) % N_GRP * SLOTS, 1), cols)
    taken = cols[NB : NB + 1] > 0.5
    col = jnp.where(taken, cols[:NB], 0.0).astype(I32)
    chunk_v[...] = col >> 3
    turn_v[...] = (((col & 7) - iota((NB, B), 0)) & 7) * K
    place_copies = [
        pltpu.make_async_copy(src, dst, sem.at[s]) for src, dst, s in ((chunk_v, chunk, 1), (turn_v, turn, 2))
    ]
    for c in place_copies:
        c.start()
    for acc in accs:
        acc[...] = jnp.zeros_like(acc)
    widths = jnp.where(taken, jnp.exp2(0.5 * widths) * (1.0 / STEPS), 0.0)
    for e in range(B):
        rows[e] = w[e // SLOTS, e % SLOTS].astype(I32).astype(F32) * widths[:, e : e + 1]
    for c in place_copies:
        c.wait()

    group = iota((K, B), 1) >> 4

    @pl.loop(0, N_GRP // 8)
    def _(j):
        for u in range(8):
            for t in range(2):
                for n in range(NB):
                    for a, acc in enumerate(accs):
                        e = j * (8 * SLOTS) + (u * SLOTS + 2 * a + t)
                        one = jnp.where(group == n, rows[e], 0.0)
                        acc[chunk[n, e]] += pltpu.roll(one, turn[n, e], 1)

    for a, acc in enumerate(accs):
        for h in range(CH):
            coarse[a, :, h * B : (h + 1) * B] = acc[h]
    copy.wait()


def on_device(q_blocks, p_blocks, col_index, agg_of_block):
    vmem, hbm, any_ = (pl.BlockSpec(memory_space=m) for m in (pltpu.VMEM, pltpu.HBM, pl.ANY))
    dma = pltpu.SemaphoreType.DMA
    inputs = (col_index.T, agg_of_block.reshape(1, R), q_blocks, p_blocks)
    prod, w_in = pl.pallas_call(
        product_kernel,
        in_specs=[hbm] * 4,
        out_specs=[vmem, any_],
        out_shape=[
            jax.ShapeDtypeStruct((R, K, B), F32),
            jax.ShapeDtypeStruct((N_GRP, SLOTS + 1, K, B), jnp.int16),
        ],
        scratch_shapes=[
            pltpu.VMEM((R, NB, B, B), BF16),
            pltpu.VMEM((3 * R, K, B), BF16),
            pltpu.VMEM((2 * R, K, B), BF16),
            pltpu.SMEM((NB, R), I32),
            pltpu.VMEM((NB, R), I32),
            pltpu.VMEM((1, R), I32),
            pltpu.VMEM((5, 8, B), F32),
            pltpu.VMEM((R, (NB - 1) * K, 2 * B), BF16),
            pltpu.VMEM((2, SLOTS, K, B), F32),
            pltpu.VMEM((N_GRP, SLOTS + 1, K, B), jnp.int16),
            pltpu.VMEM((K, B), F32),
            pltpu.VMEM((8, B), I32),
            pltpu.SMEM((8, B), I32),
            pltpu.VMEM((R, K, 2 * B), BF16),
            pltpu.VMEM((R, K, B), F32),
            dma((3,)),
            dma((6,)),
            dma((4,)),
            dma((4,)),
            dma((4,)),
            dma((4,)),
            dma((N_GRP,)),
            dma((N_GRP,)),
        ],
        compiler_params=pltpu.CompilerParams(
            collective_id=0, has_side_effects=True, vmem_limit_bytes=40 << 20
        ),
        name="products",
    )(*(pltpu.with_memory_space_constraint(x, pltpu.HBM) for x in inputs))
    coarse, product = pl.pallas_call(
        coarse_kernel,
        in_specs=[vmem, any_],
        out_specs=[vmem, any_],
        out_shape=[
            jax.ShapeDtypeStruct((OWN, K, CH * B), F32),
            jax.ShapeDtypeStruct((R, K, B), F32),
        ],
        scratch_shapes=[pltpu.VMEM((CH, K, B), F32)] * OWN
        + [pltpu.VMEM((B, K, B), F32)]
        + [pltpu.VMEM((NB, B), I32)] * 2
        + [pltpu.SMEM((NB, B), I32)] * 2
        + [dma((3,))],
        compiler_params=pltpu.CompilerParams(vmem_limit_bytes=16 << 20),
        name="coarse",
    )(w_in, prod)
    return product, coarse


def solution(mesh):
    placed = (
        P(("base", "grp"), None, None, None),
        P(("base", "grp"), None, None),
        P(("base", "grp"), None),
        P(("base", "grp"), None),
    )
    return jax.shard_map(
        on_device,
        mesh=mesh,
        in_specs=placed,
        out_specs=(P(("base", "grp"), None, None), P(("base", "grp"), None, None)),
        check_vma=False,
    )
```
